32 devices in a mesh: grp: 2 (over x), tile: 8 (over z, y), stn: 2 (over core).
Axes of the slice: x: 2, y: 2, z: 4, core: 2. Of those that a mesh axis runs over, the one named last changes fastest.
Arguments:
- samples: bfloat16 [512, 2, 126976], P(('grp', 'tile', 'stn')), parts along dimension 0, may hold values from -6 to 6
- filter_taps: float32 [16, 4096], replicated, may hold values from -1.5 to 1.5
- channel_list: int32 [768], P('grp'), parts along dimension 0, may hold values from 0 to 4095
- antenna_tile_lag: float32 [16, 512], P(None, ('grp', 'tile', 'stn')), parts along dimension 1, may hold values from -8 to 8
- tile_station_lag: float32 [16, 32], P(None, 'grp'), parts along dimension 1, may hold values from -64 to 64
- tile_of_antenna: int32 [512], P(('grp', 'tile', 'stn')), parts along dimension 0, may hold values from 0 to 15
- tile_station: int32 [32], P('grp'), parts along dimension 0, may hold values from 0 to 3, as said below
- tied_beam_pointing: int32 [2048], P('grp'), parts along dimension 0, may hold values from 0 to 15
- station_beam_lag: float32 [2048, 4], P('grp'), parts along dimension 0, may hold values from -256 to 256
Outputs:
- beam_power: float32 [2048, 384], P(('grp', 'tile', 'stn')), parts along dimension 0
The draws below stay inside these ranges and needn't reach their ends.
There are 2 independent parts, one for each index of `grp`. The reference program is written for one: setup_inputs(seed, part) draws one part's arguments, and reference() takes and returns one part's arrays. A program takes and returns all parts, laid end to end along the dimension named above; an argument that names none is the same for every part. Nothing has to cross between parts.
Inputs may be any that keep to these rules, and one draw needn't show every extreme that they name: `tile_of_antenna`: tile numbers of the group. `tile_station`: station numbers of the group; every station holds at least one tile. `channel_list`: channel numbers below 4096, repeats allowed.
All inputs are finite; a program needn't handle non-finite values.
Results may differ from the reference program's by a relative error of at most 0.0019.
Values may be sent and summed in bfloat16 or wider, within the bound.
A program may use at most 192 MiB of HBM per device.

```python
import math
import jax
import jax.numpy as jnp
from jax import lax

OUTPUT_FRAMES = 16
TAPS = 16
CH = 4096
SELECTED_COUNT = 384
POINTING_COUNT = 16
NST = 4
NB = 1024
ANTENNAS_PER_TILE = 16
GROUP_ANTENNAS = 256
GROUP_TILES = 16
TIME_SAMPLES = 126976


def draw_tile_station(key, part):
    key = jax.random.fold_in(key, 11)
    order_key, pick_key = jax.random.split(key)
    order = jax.random.permutation(order_key, GROUP_TILES).astype(jnp.int32)
    picked = jax.random.randint(pick_key, (GROUP_TILES,), 0, NST).astype(jnp.int32)
    return jnp.where(order < NST, order, picked).astype(jnp.int32)


def place_ends(entries, key, low, largest):
    longest = entries.shape.index(max(entries.shape))
    spots = []
    for shift in (0, 1):
        where = [jax.random.randint(jax.random.fold_in(key, axis), (), 0, length) for axis, length in enumerate(entries.shape)]
        where[longest] = (where[longest] + shift) % entries.shape[longest]
        spots.append(tuple(where))
    return entries.at[spots[0]].set(low).at[spots[1]].set(largest)


def block_levels(own_key, dims, cuts, low, largest):
    level, own = 1.0, jax.random.fold_in(own_key, 6)
    for position, parts in cuts:
        heights = jnp.exp(jax.random.uniform(jax.random.fold_in(own, position), (parts,), jnp.float32, low / len(cuts), largest / len(cuts)))
        level = level * jnp.repeat(heights, dims[position] // parts).reshape([-1 if axis == position else 1 for axis in range(len(dims))])
    return level


def noise(own_key, extent, spread, reach, cuts=(), kind=jnp.bfloat16):
    gain = block_levels(own_key, extent, cuts, -0.22, 0.18) if cuts else 1.0
    array = jax.random.normal(own_key, extent, jnp.float32) * spread * gain
    return jnp.minimum(jnp.maximum(array, -reach), reach).astype(kind)


def setup_inputs(seed: int = 0, part: int = 0) -> dict:
    key_list = jax.random.split(jax.random.key(seed), 10)
    own_keys = jax.random.split(jax.random.fold_in(key_list[9], part), 10)
    samples = noise(own_keys[0], (GROUP_ANTENNAS, 2, TIME_SAMPLES), 1.0, 6.0, ((0, 16),))
    filter_taps = noise(key_list[1], (TAPS, CH), 0.25, 1.5, (), jnp.float32)
    channel_list = place_ends(jax.random.randint(own_keys[2], (SELECTED_COUNT,), 0, CH), jax.random.fold_in(own_keys[2], 1), 0, CH - 1).astype(jnp.int32)
    antenna_tile_lag = jnp.clip(jax.random.uniform(own_keys[3], (POINTING_COUNT, GROUP_ANTENNAS), jnp.float32, -8.0, 8.0) * block_levels(own_keys[3], (POINTING_COUNT, GROUP_ANTENNAS), ((1, 16),), -0.4, 0.0), -8.0, 8.0)
    tile_station_lag = jnp.clip(jax.random.uniform(own_keys[4], (POINTING_COUNT, GROUP_TILES), jnp.float32, -64.0, 64.0), -64.0, 64.0)
    tile_of_antenna = place_ends(jax.random.randint(own_keys[5], (GROUP_ANTENNAS,), 0, GROUP_TILES), jax.random.fold_in(own_keys[5], 1), 0, GROUP_TILES - 1).astype(jnp.int32)
    tile_station = draw_tile_station(jax.random.fold_in(jax.random.fold_in(key_list[9], part), 71), part)
    tied_beam_pointing = place_ends(jax.random.randint(own_keys[7], (NB,), 0, POINTING_COUNT), jax.random.fold_in(own_keys[7], 1), 0, POINTING_COUNT - 1).astype(jnp.int32)
    station_beam_lag = jnp.clip(jax.random.uniform(own_keys[8], (NB, NST), jnp.float32, -256.0, 256.0), -256.0, 256.0)
    return {"samples": samples, "filter_taps": filter_taps, "channel_list": channel_list, "antenna_tile_lag": antenna_tile_lag, "tile_station_lag": tile_station_lag, "tile_of_antenna": tile_of_antenna, "tile_station": tile_station, "tied_beam_pointing": tied_beam_pointing, "station_beam_lag": station_beam_lag}


TWO_PI = 6.283185307179586

def keep_selected(values):
    rounded = lax.optimization_barrier(values.astype(jnp.bfloat16))
    return rounded.astype(jnp.float32)

def filter_bank(samples, filter_taps):
    num_taps, channels = filter_taps.shape
    frames = samples.shape[2] // channels - num_taps + 1
    blocks = samples.reshape(samples.shape[0], 2, frames + num_taps - 1, channels)
    filtered = blocks[:, :, 0:frames, :] * filter_taps[0]
    for tap_index in range(1, num_taps):
        filtered = filtered + blocks[:, :, tap_index:tap_index + frames, :] * filter_taps[tap_index]
    return filtered

def dft_table(channel_list, channels):
    sample_idx = lax.broadcasted_iota(jnp.int32, (channels, channel_list.shape[0]), 0)
    turn_count = sample_idx * channel_list[None, :] % channels
    angles = turn_count.astype(jnp.float32) * (TWO_PI / channels)
    factor = 1.0 / math.sqrt(channels)
    cosine = jnp.cos(angles) * factor
    sine_part = jnp.sin(angles) * factor
    upper_half = jnp.concatenate([cosine, -sine_part], axis=1)
    lower_half = jnp.concatenate([sine_part, cosine], axis=1)
    return jnp.stack([upper_half, lower_half])

def station_weight_matrix(antenna_lag, tile_indicator, frequency_radians):
    phase_angles = antenna_lag[:, :, None] * frequency_radians[None, None, :]
    cosine = jnp.cos(phase_angles)
    sine_part = jnp.sin(phase_angles)
    real_rows = jnp.stack([cosine, sine_part], axis=1)
    imag_rows = jnp.stack([-sine_part, cosine], axis=1)
    stacked_spectra = jnp.stack([real_rows, imag_rows], axis=1)
    weight_matrix = tile_indicator[:, None, None, None, :, None] * stacked_spectra[None]
    return weight_matrix.reshape((tile_indicator.shape[0] * antenna_lag.shape[0],) + stacked_spectra.shape[1:])

def tied_beam_power(station_beam_output, pointing, beam_delay, frequency_radians, factor):
    chosen = jnp.take(station_beam_output, pointing, axis=3)
    angles = beam_delay.T[None, :, :] * frequency_radians[:, None, None]
    cosine = jnp.cos(angles)[..., None]
    sine_part = jnp.sin(angles)[..., None]
    real_part = lax.optimization_barrier(jnp.sum(chosen[:, 0] * cosine + chosen[:, 1] * sine_part, axis=1))
    imag_part = lax.optimization_barrier(jnp.sum(chosen[:, 1] * cosine - chosen[:, 0] * sine_part, axis=1))
    powers = lax.optimization_barrier(jnp.sum(real_part * real_part + imag_part * imag_part, axis=2)) * factor
    return powers.T

def reference(samples, filter_taps, channel_list, antenna_tile_lag, tile_station_lag, tile_of_antenna, tile_station, tied_beam_pointing, station_beam_lag):
    channels = filter_taps.shape[1]
    dft_rows = keep_selected(dft_table(channel_list, channels))
    antenna_groups = samples.reshape(GROUP_ANTENNAS // ANTENNAS_PER_TILE, ANTENNAS_PER_TILE, 2, samples.shape[2])

    def split_into_channels(antenna_group):
        filtered = keep_selected(filter_bank(antenna_group, filter_taps))
        channel_spectra = jnp.einsum('arfn,rnk->afk', filtered, dft_rows, precision=lax.Precision.HIGHEST)
        return keep_selected(channel_spectra)
    channel_spectra = lax.map(split_into_channels, antenna_groups).reshape(GROUP_ANTENNAS, OUTPUT_FRAMES, 2, SELECTED_COUNT)
    antenna_lag = antenna_tile_lag + tile_station_lag[:, tile_of_antenna]
    station = tile_station[tile_of_antenna]
    tile_indicator = (station[None, :] == jnp.arange(NST, dtype=jnp.int32)[:, None]).astype(jnp.float32)
    frequency_radians = channel_list.astype(jnp.float32) * (TWO_PI / channels)
    block_size = math.gcd(SELECTED_COUNT, 64)

    def station_block(first_channel):
        frequency_piece = lax.dynamic_slice_in_dim(frequency_radians, first_channel, block_size)
        volt_part = lax.dynamic_slice_in_dim(channel_spectra, first_channel, block_size, 3)
        weight_matrix = keep_selected(station_weight_matrix(antenna_lag, tile_indicator, frequency_piece))
        return jnp.einsum('qorac,afrc->coqf', weight_matrix, volt_part, precision=lax.Precision.HIGHEST)
    starts = jnp.arange(SELECTED_COUNT // block_size, dtype=jnp.int32) * block_size
    station_beam_output = lax.map(station_block, starts).reshape(SELECTED_COUNT, 2, NST, POINTING_COUNT, OUTPUT_FRAMES)
    return tied_beam_power(station_beam_output, tied_beam_pointing, station_beam_lag, frequency_radians, 1.0 / (OUTPUT_FRAMES * GROUP_ANTENNAS))
```

```python
import functools
import itertools
import math

import jax
import jax.numpy as jnp
from jax import lax
from jax.experimental import pallas as pl
from jax.experimental.pallas import tpu as pltpu
from jax.sharding import PartitionSpec as P

TWO_PI = 6.283185307179586
LANES = 128
CHUNK = 512
GROUP_AXES = ("tile", "stn")


def filter_dft_kernel(frames, taps, x_ref, taps_ref, ca_ref, sa_ref, cb_ref, sb_ref, out_ref, filt, table, acc):
    step = pl.program_id(0)
    antennas = x_ref.shape[2]
    selected = cb_ref.shape[0]
    rows = frames * antennas

    for piece in range(CHUNK // LANES):
        lanes = slice(piece * LANES, (piece + 1) * LANES)
        ca = ca_ref[0, :, piece : piece + 1]
        sa = sa_ref[0, :, piece : piece + 1]
        cb = cb_ref[...]
        sb = sb_ref[...]
        table[0:selected, lanes] = (ca * cb - sa * sb).astype(jnp.bfloat16)
        table[selected : 2 * selected, lanes] = (sa * cb + ca * sb).astype(jnp.bfloat16)
        weights = [
            jnp.broadcast_to(taps_ref[j : j + 1, lanes], (antennas, LANES)) for j in range(taps)
        ]
        for r in range(2):
            blocks = [
                x_ref[k, r, :, lanes].astype(jnp.float32) for k in range(frames + taps - 1)
            ]
            for f in range(frames):
                total = blocks[f] * weights[0]
                for j in range(1, taps):
                    total = total + blocks[f + j] * weights[j]
                start = r * rows + f * antennas
                filt[start : start + antennas, lanes] = total.astype(jnp.bfloat16)

    product = lax.dot_general(
        table[...], filt[...], (((1,), (1,)), ((), ())), preferred_element_type=jnp.float32
    )

    @pl.when(step == 0)
    def _():
        acc[...] = product

    @pl.when(step > 0)
    def _():
        acc[...] += product

    @pl.when(step == pl.num_programs(0) - 1)
    def _():
        out_ref[:, 0:rows] = (
            acc[0:selected, 0:rows] + acc[selected : 2 * selected, rows : 2 * rows]
        ).astype(jnp.bfloat16)
        out_ref[:, rows : 2 * rows] = (
            acc[0:selected, rows : 2 * rows] - acc[selected : 2 * selected, 0:rows]
        ).astype(jnp.bfloat16)


def unit_tables(sample_idx, channel_list, channels, factor):
    turn_count = sample_idx * channel_list[:, None] % channels
    angles = turn_count.astype(jnp.float32) * (TWO_PI / channels)
    return jnp.cos(angles) * factor, jnp.sin(angles) * factor


def channel_spectra(samples, filter_taps, channel_list):
    taps, channels = filter_taps.shape
    antennas = samples.shape[0]
    selected = channel_list.shape[0]
    blocks = samples.shape[2] // channels
    frames = blocks - taps + 1
    steps = channels // CHUNK
    pieces = CHUNK // LANES
    x = samples.reshape(antennas, 2, blocks, channels).transpose(2, 1, 0, 3)
    coarse = lax.broadcasted_iota(jnp.int32, (selected, channels // LANES), 1) * LANES
    fine = lax.broadcasted_iota(jnp.int32, (selected, LANES), 1)
    ca, sa = unit_tables(coarse, channel_list, channels, 1.0 / math.sqrt(channels))
    cb, sb = unit_tables(fine, channel_list, channels, 1.0)
    ca = ca.reshape(selected, steps, pieces).transpose(1, 0, 2)
    sa = sa.reshape(selected, steps, pieces).transpose(1, 0, 2)
    width = 2 * frames * antennas
    return pl.pallas_call(
        functools.partial(filter_dft_kernel, frames, taps),
        grid=(steps,),
        in_specs=[
            pl.BlockSpec((blocks, 2, antennas, CHUNK), lambda i: (0, 0, 0, i)),
            pl.BlockSpec((taps, CHUNK), lambda i: (0, i)),
            pl.BlockSpec((1, selected, pieces), lambda i: (i, 0, 0)),
            pl.BlockSpec((1, selected, pieces), lambda i: (i, 0, 0)),
            pl.BlockSpec((selected, LANES), lambda i: (0, 0)),
            pl.BlockSpec((selected, LANES), lambda i: (0, 0)),
        ],
        out_specs=pl.BlockSpec((selected, width), lambda i: (0, 0)),
        out_shape=jax.ShapeDtypeStruct((selected, width), jnp.bfloat16),
        scratch_shapes=[
            pltpu.VMEM((width, CHUNK), jnp.bfloat16),
            pltpu.VMEM((2 * selected, CHUNK), jnp.bfloat16),
            pltpu.VMEM((2 * selected, width), jnp.float32),
        ],
        compiler_params=pltpu.CompilerParams(vmem_limit_bytes=32 * 1024 * 1024),
    )(x, filter_taps, ca, sa, cb, sb)


def antenna_info(antenna_tile_lag, tile_station_lag, tile_of_antenna, tile_station):
    tile_ids = jnp.arange(tile_station_lag.shape[1], dtype=jnp.int32)
    matches = tile_of_antenna[:, None] == tile_ids[None, :]
    extra = jnp.sum(jnp.where(matches[None, :, :], tile_station_lag[:, None, :], 0.0), axis=2)
    station = jnp.sum(jnp.where(matches, tile_station[None, :], 0), axis=1)
    return jnp.concatenate([antenna_tile_lag + extra, station.astype(jnp.float32)[None]], axis=0)


def body(
    samples,
    filter_taps,
    channel_list,
    antenna_tile_lag,
    tile_station_lag,
    tile_of_antenna,
    tile_station,
    tied_beam_pointing,
    station_beam_lag,
):
    devices = lax.axis_size(GROUP_AXES)
    own_rank = lax.axis_index(GROUP_AXES)
    taps, channels = filter_taps.shape
    frames = samples.shape[2] // channels - taps + 1
    stations = station_beam_lag.shape[1]
    pointings = tile_station_lag.shape[0]
    selected = channel_list.shape[0]
    antennas = samples.shape[0]
    share = selected // devices
    beams = tied_beam_pointing.shape[0]

    info = antenna_info(antenna_tile_lag, tile_station_lag, tile_of_antenna, tile_station)
    info = lax.all_gather(info, GROUP_AXES, axis=1, tiled=True)
    lag = info[:pointings]
    mask = (
        info[pointings][None, :] == jnp.arange(stations, dtype=jnp.float32)[:, None]
    ).astype(jnp.bfloat16)

    own_channels = lax.dynamic_slice_in_dim(channel_list, own_rank * share, share)
    omega = own_channels.astype(jnp.float32) * (TWO_PI / channels)
    angles = lag[None] * omega[:, None, None]
    weights = jnp.concatenate([jnp.cos(angles), jnp.sin(angles)], axis=1).astype(jnp.bfloat16)
    theta = station_beam_lag.T[:, None, :] * omega[None, :, None]
    cosine = jnp.cos(theta)
    sine = jnp.sin(theta)
    onehot = (
        tied_beam_pointing[None, :] == jnp.arange(pointings, dtype=jnp.int32)[:, None]
    ).astype(jnp.float32)

    spectra = channel_spectra(samples, filter_taps, channel_list)
    spectra = lax.all_to_all(spectra, GROUP_AXES, split_axis=0, concat_axis=0, tiled=True)
    spectra = spectra.reshape(devices, share, 2 * frames, antennas).transpose(1, 2, 0, 3)
    spectra = spectra.reshape(share, 1, 2 * frames, devices * antennas)
    masked = (spectra * mask[None, :, None, :]).reshape(
        share, stations * 2 * frames, devices * antennas
    )
    terms = jnp.einsum("cua,cva->cuv", weights, masked, preferred_element_type=jnp.float32)
    terms = terms.reshape(share, 2, pointings, stations, 2, frames)
    real = terms[:, 0, :, :, 0] + terms[:, 1, :, :, 1]
    imag = terms[:, 0, :, :, 1] - terms[:, 1, :, :, 0]

    factor = 1.0 / (frames * antennas * devices)
    pairs = list(itertools.combinations(range(stations), 2))
    moments = [jnp.sum(real * real + imag * imag, axis=(2, 3)) * factor]
    for s, t in pairs:
        moments.append(
            jnp.sum(real[:, :, s] * real[:, :, t] + imag[:, :, s] * imag[:, :, t], axis=2)
            * (2.0 * factor)
        )
    for s, t in pairs:
        moments.append(
            jnp.sum(imag[:, :, s] * real[:, :, t] - real[:, :, s] * imag[:, :, t], axis=2)
            * (2.0 * factor)
        )
    moments = jnp.stack(moments).reshape(len(moments) * share, pointings)
    chosen = jnp.dot(moments, onehot, precision=lax.Precision.HIGHEST).reshape(-1, share, beams)
    power = chosen[0]
    for i, (s, t) in enumerate(pairs):
        power = power + chosen[1 + i] * (cosine[s] * cosine[t] + sine[s] * sine[t])
        power = power + chosen[1 + len(pairs) + i] * (sine[s] * cosine[t] - cosine[s] * sine[t])
    power = lax.all_to_all(power, GROUP_AXES, split_axis=1, concat_axis=0, tiled=True)
    return power.T


def solution(mesh):
    in_specs = (
        P(("grp", "tile", "stn"), None, None),
        P(),
        P("grp"),
        P(None, ("grp", "tile", "stn")),
        P(None, "grp"),
        P(("grp", "tile", "stn")),
        P("grp"),
        P("grp"),
        P("grp", None),
    )
    out_specs = P(("grp", "tile", "stn"), None)
    return jax.shard_map(body, mesh=mesh, in_specs=in_specs, out_specs=out_specs, check_vma=False)
```

```python
import functools
import itertools
import math

import jax
import jax.numpy as jnp
from jax import lax
from jax.experimental import pallas as pl
from jax.experimental.pallas import tpu as pltpu
from jax.sharding import PartitionSpec as P

TWO_PI = 6.283185307179586
LANES = 128
CHUNK = 512
GROUP_AXES = ("tile", "stn")


def filter_dft_kernel(frames, taps, x_ref, taps_ref, ca_ref, sa_ref, cb_ref, sb_ref, extra_ref, out_ref, filt, table, acc):
    step = pl.program_id(0)
    antennas = x_ref.shape[2]
    selected = cb_ref.shape[0]
    rows = frames * antennas

    for piece in range(CHUNK // LANES):
        lanes = slice(piece * LANES, (piece + 1) * LANES)
        ca = ca_ref[0, :, piece : piece + 1]
        sa = sa_ref[0, :, piece : piece + 1]
        cb = cb_ref[...]
        sb = sb_ref[...]
        table[0:selected, lanes] = (ca * cb - sa * sb).astype(jnp.bfloat16)
        table[selected : 2 * selected, lanes] = (sa * cb + ca * sb).astype(jnp.bfloat16)
        weights = [
            jnp.broadcast_to(taps_ref[j : j + 1, lanes], (antennas, LANES)) for j in range(taps)
        ]
        for r in range(2):
            blocks = [
                x_ref[k, r, :, lanes].astype(jnp.float32) for k in range(frames + taps - 1)
            ]
            for f in range(frames):
                total = blocks[f] * weights[0]
                for j in range(1, taps):
                    total = total + blocks[f + j] * weights[j]
                start = r * rows + f * antennas
                filt[start : start + antennas, lanes] = total.astype(jnp.bfloat16)

    product = lax.dot_general(
        table[...], filt[...], (((1,), (1,)), ((), ())), preferred_element_type=jnp.float32
    )

    @pl.when(step == 0)
    def _():
        acc[...] = product

    @pl.when(step > 0)
    def _():
        acc[...] += product

    @pl.when(step == pl.num_programs(0) - 1)
    def _():
        out_ref[:, 2 * rows :] = extra_ref[...]
        out_ref[:, 0:rows] = (
            acc[0:selected, 0:rows] + acc[selected : 2 * selected, rows : 2 * rows]
        ).astype(jnp.bfloat16)
        out_ref[:, rows : 2 * rows] = (
            acc[0:selected, rows : 2 * rows] - acc[selected : 2 * selected, 0:rows]
        ).astype(jnp.bfloat16)


def unit_tables(sample_idx, channel_list, channels, factor):
    turn_count = sample_idx * channel_list[:, None] % channels
    angles = turn_count.astype(jnp.float32) * (TWO_PI / channels)
    return jnp.cos(angles) * factor, jnp.sin(angles) * factor


def channel_spectra(samples, filter_taps, channel_list, extra):
    taps, channels = filter_taps.shape
    antennas = samples.shape[0]
    selected = channel_list.shape[0]
    blocks = samples.shape[2] // channels
    frames = blocks - taps + 1
    steps = channels // CHUNK
    pieces = CHUNK // LANES
    x = samples.reshape(antennas, 2, blocks, channels).transpose(2, 1, 0, 3)
    coarse = lax.broadcasted_iota(jnp.int32, (selected, channels // LANES), 1) * LANES
    fine = lax.broadcasted_iota(jnp.int32, (selected, LANES), 1)
    ca, sa = unit_tables(coarse, channel_list, channels, 1.0 / math.sqrt(channels))
    cb, sb = unit_tables(fine, channel_list, channels, 1.0)
    ca = ca.reshape(selected, steps, pieces).transpose(1, 0, 2)
    sa = sa.reshape(selected, steps, pieces).transpose(1, 0, 2)
    width = 2 * frames * antennas
    return pl.pallas_call(
        functools.partial(filter_dft_kernel, frames, taps),
        grid=(steps,),
        in_specs=[
            pl.BlockSpec((blocks, 2, antennas, CHUNK), lambda i: (0, 0, 0, i)),
            pl.BlockSpec((taps, CHUNK), lambda i: (0, i)),
            pl.BlockSpec((1, selected, pieces), lambda i: (i, 0, 0)),
            pl.BlockSpec((1, selected, pieces), lambda i: (i, 0, 0)),
            pl.BlockSpec((selected, LANES), lambda i: (0, 0)),
            pl.BlockSpec((selected, LANES), lambda i: (0, 0)),
            pl.BlockSpec(extra.shape, lambda i: (0, 0)),
        ],
        out_specs=pl.BlockSpec((selected, width + extra.shape[1]), lambda i: (0, 0)),
        out_shape=jax.ShapeDtypeStruct((selected, width + extra.shape[1]), jnp.bfloat16),
        scratch_shapes=[
            pltpu.VMEM((width, CHUNK), jnp.bfloat16),
            pltpu.VMEM((2 * selected, CHUNK), jnp.bfloat16),
            pltpu.VMEM((2 * selected, width), jnp.float32),
        ],
        compiler_params=pltpu.CompilerParams(vmem_limit_bytes=32 * 1024 * 1024),
    )(x, filter_taps, ca, sa, cb, sb, extra)


def beam_power_kernel(frames, factor, x_ref, w_ref, mask_ref, cos_ref, sin_ref, onehot_ref, out_ref, moments):
    share = x_ref.shape[0]
    stations = mask_ref.shape[0]
    pointings = onehot_ref.shape[0]
    pairs = list(itertools.combinations(range(stations), 2))
    for c in range(share):
        x = x_ref[c].astype(jnp.float32)
        real, imag = [], []
        for s in range(stations):
            masked = (x * mask_ref[s : s + 1, :]).astype(jnp.bfloat16)
            terms = lax.dot_general(
                masked, w_ref[c], (((1,), (1,)), ((), ())), preferred_element_type=jnp.float32
            )
            cos_part = terms[:, 0:pointings]
            sin_part = terms[:, pointings : 2 * pointings]
            real.append(cos_part[0:frames] + sin_part[frames : 2 * frames])
            imag.append(cos_part[frames : 2 * frames] - sin_part[0:frames])
        total = real[0] * real[0] + imag[0] * imag[0]
        for s in range(1, stations):
            total = total + (real[s] * real[s] + imag[s] * imag[s])
        moments[0, c : c + 1, :] = jnp.sum(total, axis=0, keepdims=True) * factor
        for i, (s, t) in enumerate(pairs):
            even = real[s] * real[t] + imag[s] * imag[t]
            odd = imag[s] * real[t] - real[s] * imag[t]
            moments[1 + i, c : c + 1, :] = jnp.sum(even, axis=0, keepdims=True) * (2.0 * factor)
            moments[1 + len(pairs) + i, c : c + 1, :] = jnp.sum(odd, axis=0, keepdims=True) * (
                2.0 * factor
            )

    def chosen(m):
        return jnp.dot(
            moments[m],
            onehot_ref[...],
            precision=lax.Precision.HIGHEST,
            preferred_element_type=jnp.float32,
        )

    power = chosen(0)
    for i, (s, t) in enumerate(pairs):
        power = power + chosen(1 + i) * (cos_ref[s] * cos_ref[t] + sin_ref[s] * sin_ref[t])
        power = power + chosen(1 + len(pairs) + i) * (
            sin_ref[s] * cos_ref[t] - cos_ref[s] * sin_ref[t]
        )
    beams = out_ref.shape[2]
    for d in range(out_ref.shape[0]):
        out_ref[d] = power[:, d * beams : (d + 1) * beams]


def split_rows(values):
    first = lax.reduce_precision(values, 8, 7)
    second = lax.reduce_precision(values - first, 8, 7)
    third = values - first - second
    return jnp.stack([first, second, third], axis=1).astype(jnp.bfloat16)


def antenna_info(antenna_tile_lag, tile_station_lag, tile_of_antenna, tile_station):
    tile_ids = jnp.arange(tile_station_lag.shape[1], dtype=jnp.int32)
    matches = tile_of_antenna[:, None] == tile_ids[None, :]
    extra = jnp.sum(jnp.where(matches[None, :, :], tile_station_lag[:, None, :], 0.0), axis=2)
    station = jnp.sum(jnp.where(matches, tile_station[None, :], 0), axis=1)
    return jnp.concatenate([antenna_tile_lag + extra, station.astype(jnp.float32)[None]], axis=0)


def body(
    samples,
    filter_taps,
    channel_list,
    antenna_tile_lag,
    tile_station_lag,
    tile_of_antenna,
    tile_station,
    tied_beam_pointing,
    station_beam_lag,
):
    devices = lax.axis_size(GROUP_AXES)
    own_rank = lax.axis_index(GROUP_AXES)
    taps, channels = filter_taps.shape
    frames = samples.shape[2] // channels - taps + 1
    stations = station_beam_lag.shape[1]
    pointings = tile_station_lag.shape[0]
    selected = channel_list.shape[0]
    antennas = samples.shape[0]
    share = selected // devices
    beams = tied_beam_pointing.shape[0]

    info = antenna_info(antenna_tile_lag, tile_station_lag, tile_of_antenna, tile_station)
    info_rows = info.shape[0]
    groups = -(-info_rows // share)
    pieces = split_rows(info)
    pieces = jnp.pad(pieces, ((0, groups * share - info_rows), (0, 0), (0, 0)))
    pieces = pieces.reshape(groups, share, 3 * antennas).transpose(1, 0, 2)
    pieces = pieces.reshape(share, groups * 3 * antennas)
    extra_width = -(-pieces.shape[1] // LANES) * LANES
    pieces = jnp.pad(pieces, ((0, 0), (0, extra_width - pieces.shape[1])))
    extra = jnp.tile(pieces, (devices, 1))

    own_channels = lax.dynamic_slice_in_dim(channel_list, own_rank * share, share)
    omega = own_channels.astype(jnp.float32) * (TWO_PI / channels)
    theta = station_beam_lag.T[:, None, :] * omega[None, :, None]
    cosine = jnp.cos(theta)
    sine = jnp.sin(theta)
    onehot = (
        tied_beam_pointing[None, :] == jnp.arange(pointings, dtype=jnp.int32)[:, None]
    ).astype(jnp.float32)

    spectra = channel_spectra(samples, filter_taps, channel_list, extra)
    spectra = lax.all_to_all(spectra, GROUP_AXES, split_axis=0, concat_axis=0, tiled=True)
    width = 2 * frames * antennas
    total = devices * antennas

    pieces = spectra[:, width : width + groups * 3 * antennas].astype(jnp.float32)
    pieces = pieces.reshape(devices, share, groups, 3, antennas)
    info = (pieces[:, :, :, 0] + pieces[:, :, :, 1]) + pieces[:, :, :, 2]
    info = info.transpose(2, 1, 0, 3).reshape(groups * share, total)
    lag = info[:pointings]
    mask = (
        info[pointings][None, :] == jnp.arange(stations, dtype=jnp.float32)[:, None]
    ).astype(jnp.float32)
    angles = lag[None] * omega[:, None, None]
    weights = jnp.concatenate([jnp.cos(angles), jnp.sin(angles)], axis=1).astype(jnp.bfloat16)

    spectra = spectra[:, :width].reshape(devices, share, 2 * frames, antennas)
    spectra = spectra.transpose(1, 2, 0, 3).reshape(share, 2 * frames, total)
    moment_count = stations * stations - stations + 1
    power = pl.pallas_call(
        functools.partial(beam_power_kernel, frames, 1.0 / (frames * total)),
        out_shape=jax.ShapeDtypeStruct((devices, share, beams // devices), jnp.float32),
        scratch_shapes=[pltpu.VMEM((moment_count, share, pointings), jnp.float32)],
        compiler_params=pltpu.CompilerParams(vmem_limit_bytes=32 * 1024 * 1024),
    )(spectra, weights, mask, cosine, sine, onehot)
    power = lax.all_to_all(power, GROUP_AXES, split_axis=0, concat_axis=0, tiled=True)
    return power.reshape(selected, beams // devices).T


def solution(mesh):
    in_specs = (
        P(("grp", "tile", "stn"), None, None),
        P(),
        P("grp"),
        P(None, ("grp", "tile", "stn")),
        P(None, "grp"),
        P(("grp", "tile", "stn")),
        P("grp"),
        P("grp"),
        P("grp", None),
    )
    out_specs = P(("grp", "tile", "stn"), None)
    return jax.shard_map(body, mesh=mesh, in_specs=in_specs, out_specs=out_specs, check_vma=False)
```

```python
import functools
import itertools
import math

import jax
import jax.numpy as jnp
from jax import lax
from jax.experimental import pallas as pl
from jax.experimental.pallas import tpu as pltpu
from jax.sharding import PartitionSpec as P

TWO_PI = 6.283185307179586
LANES = 128
CHUNK = 512
GROUP_AXES = ("tile", "stn")


def filter_dft_kernel(frames, taps, x_ref, taps_ref, ca_ref, sa_ref, cb_ref, sb_ref, extra_ref, out_ref, filt, table, acc):
    step = pl.program_id(0)
    antennas = x_ref.shape[0]
    selected = cb_ref.shape[0]
    rows = frames * antennas

    for piece in range(CHUNK // LANES):
        lanes = slice(piece * LANES, (piece + 1) * LANES)
        ca = ca_ref[0, :, piece : piece + 1]
        sa = sa_ref[0, :, piece : piece + 1]
        cb = cb_ref[...]
        sb = sb_ref[...]
        table[0:selected, lanes] = (ca * cb - sa * sb).astype(jnp.bfloat16)
        table[selected : 2 * selected, lanes] = (sa * cb + ca * sb).astype(jnp.bfloat16)
        weights = [
            jnp.broadcast_to(taps_ref[j : j + 1, lanes], (antennas, LANES)) for j in range(taps)
        ]
        for r in range(2):
            blocks = [
                x_ref[:, k, r, lanes].astype(jnp.float32) for k in range(frames + taps - 1)
            ]
            for f in range(frames):
                total = blocks[f] * weights[0]
                for j in range(1, taps):
                    total = total + blocks[f + j] * weights[j]
                start = r * rows + f * antennas
                filt[start : start + antennas, lanes] = total.astype(jnp.bfloat16)

    product = lax.dot_general(
        table[...], filt[...], (((1,), (1,)), ((), ())), preferred_element_type=jnp.float32
    )

    @pl.when(step == 0)
    def _():
        acc[...] = product

    @pl.when(step > 0)
    def _():
        acc[...] += product

    @pl.when(step == pl.num_programs(0) - 1)
    def _():
        out_ref[:, 2 * rows :] = extra_ref[...]
        out_ref[:, 0:rows] = (
            acc[0:selected, 0:rows] + acc[selected : 2 * selected, rows : 2 * rows]
        ).astype(jnp.bfloat16)
        out_ref[:, rows : 2 * rows] = (
            acc[0:selected, rows : 2 * rows] - acc[selected : 2 * selected, 0:rows]
        ).astype(jnp.bfloat16)


def unit_tables(sample_idx, channel_list, channels, factor):
    turn_count = sample_idx * channel_list[:, None] % channels
    angles = turn_count.astype(jnp.float32) * (TWO_PI / channels)
    return jnp.cos(angles) * factor, jnp.sin(angles) * factor


def channel_spectra(samples, filter_taps, channel_list, extra):
    taps, channels = filter_taps.shape
    antennas = samples.shape[0]
    selected = channel_list.shape[0]
    blocks = samples.shape[2] // channels
    frames = blocks - taps + 1
    steps = channels // CHUNK
    pieces = CHUNK // LANES
    x = samples.reshape(antennas, 2, blocks, channels).transpose(0, 2, 1, 3)
    coarse = lax.broadcasted_iota(jnp.int32, (selected, channels // LANES), 1) * LANES
    fine = lax.broadcasted_iota(jnp.int32, (selected, LANES), 1)
    ca, sa = unit_tables(coarse, channel_list, channels, 1.0 / math.sqrt(channels))
    cb, sb = unit_tables(fine, channel_list, channels, 1.0)
    ca = ca.reshape(selected, steps, pieces).transpose(1, 0, 2)
    sa = sa.reshape(selected, steps, pieces).transpose(1, 0, 2)
    width = 2 * frames * antennas
    return pl.pallas_call(
        functools.partial(filter_dft_kernel, frames, taps),
        grid=(steps,),
        in_specs=[
            pl.BlockSpec((antennas, blocks, 2, CHUNK), lambda i: (0, 0, 0, i)),
            pl.BlockSpec((taps, CHUNK), lambda i: (0, i)),
            pl.BlockSpec((1, selected, pieces), lambda i: (i, 0, 0)),
            pl.BlockSpec((1, selected, pieces), lambda i: (i, 0, 0)),
            pl.BlockSpec((selected, LANES), lambda i: (0, 0)),
            pl.BlockSpec((selected, LANES), lambda i: (0, 0)),
            pl.BlockSpec(extra.shape, lambda i: (0, 0)),
        ],
        out_specs=pl.BlockSpec((selected, width + extra.shape[1]), lambda i: (0, 0)),
        out_shape=jax.ShapeDtypeStruct((selected, width + extra.shape[1]), jnp.bfloat16),
        scratch_shapes=[
            pltpu.VMEM((width, CHUNK), jnp.bfloat16),
            pltpu.VMEM((2 * selected, CHUNK), jnp.bfloat16),
            pltpu.VMEM((2 * selected, width), jnp.float32),
        ],
        compiler_params=pltpu.CompilerParams(vmem_limit_bytes=32 * 1024 * 1024),
    )(x, filter_taps, ca, sa, cb, sb, extra)


def beam_power_kernel(frames, factor, x_ref, w_ref, mask_ref, cos_ref, sin_ref, onehot_ref, out_ref, moments):
    share = x_ref.shape[0]
    stations = mask_ref.shape[0]
    pointings = onehot_ref.shape[0]
    pairs = list(itertools.combinations(range(stations), 2))
    for c in range(share):
        x = x_ref[c].astype(jnp.float32)
        real, imag = [], []
        for s in range(stations):
            masked = (x * mask_ref[s : s + 1, :]).astype(jnp.bfloat16)
            terms = lax.dot_general(
                masked, w_ref[c], (((1,), (1,)), ((), ())), preferred_element_type=jnp.float32
            )
            cos_part = terms[:, 0:pointings]
            sin_part = terms[:, pointings : 2 * pointings]
            real.append(cos_part[0:frames] + sin_part[frames : 2 * frames])
            imag.append(cos_part[frames : 2 * frames] - sin_part[0:frames])
        total = real[0] * real[0] + imag[0] * imag[0]
        for s in range(1, stations):
            total = total + (real[s] * real[s] + imag[s] * imag[s])
        moments[0, c : c + 1, :] = jnp.sum(total, axis=0, keepdims=True) * factor
        for i, (s, t) in enumerate(pairs):
            even = real[s] * real[t] + imag[s] * imag[t]
            odd = imag[s] * real[t] - real[s] * imag[t]
            moments[1 + i, c : c + 1, :] = jnp.sum(even, axis=0, keepdims=True) * (2.0 * factor)
            moments[1 + len(pairs) + i, c : c + 1, :] = jnp.sum(odd, axis=0, keepdims=True) * (
                2.0 * factor
            )

    def chosen(m):
        return jnp.dot(
            moments[m],
            onehot_ref[...],
            precision=lax.Precision.HIGHEST,
            preferred_element_type=jnp.float32,
        )

    power = chosen(0)
    for i, (s, t) in enumerate(pairs):
        power = power + chosen(1 + i) * (cos_ref[s] * cos_ref[t] + sin_ref[s] * sin_ref[t])
        power = power + chosen(1 + len(pairs) + i) * (
            sin_ref[s] * cos_ref[t] - cos_ref[s] * sin_ref[t]
        )
    beams = out_ref.shape[2]
    for d in range(out_ref.shape[0]):
        out_ref[d] = power[:, d * beams : (d + 1) * beams]


def split_rows(values):
    first = lax.reduce_precision(values, 8, 7)
    second = lax.reduce_precision(values - first, 8, 7)
    third = values - first - second
    return jnp.stack([first, second, third], axis=1).astype(jnp.bfloat16)


def antenna_info(antenna_tile_lag, tile_station_lag, tile_of_antenna, tile_station):
    tile_ids = jnp.arange(tile_station_lag.shape[1], dtype=jnp.int32)
    matches = tile_of_antenna[:, None] == tile_ids[None, :]
    extra = jnp.sum(jnp.where(matches[None, :, :], tile_station_lag[:, None, :], 0.0), axis=2)
    station = jnp.sum(jnp.where(matches, tile_station[None, :], 0), axis=1)
    return jnp.concatenate([antenna_tile_lag + extra, station.astype(jnp.float32)[None]], axis=0)


def body(
    samples,
    filter_taps,
    channel_list,
    antenna_tile_lag,
    tile_station_lag,
    tile_of_antenna,
    tile_station,
    tied_beam_pointing,
    station_beam_lag,
):
    devices = lax.axis_size(GROUP_AXES)
    own_rank = lax.axis_index(GROUP_AXES)
    taps, channels = filter_taps.shape
    frames = samples.shape[2] // channels - taps + 1
    stations = station_beam_lag.shape[1]
    pointings = tile_station_lag.shape[0]
    selected = channel_list.shape[0]
    antennas = samples.shape[0]
    share = selected // devices
    beams = tied_beam_pointing.shape[0]

    info = antenna_info(antenna_tile_lag, tile_station_lag, tile_of_antenna, tile_station)
    info_rows = info.shape[0]
    groups = -(-info_rows // share)
    pieces = split_rows(info)
    pieces = jnp.pad(pieces, ((0, groups * share - info_rows), (0, 0), (0, 0)))
    pieces = pieces.reshape(groups, share, 3 * antennas).transpose(1, 0, 2)
    pieces = pieces.reshape(share, groups * 3 * antennas)
    extra_width = -(-pieces.shape[1] // LANES) * LANES
    pieces = jnp.pad(pieces, ((0, 0), (0, extra_width - pieces.shape[1])))
    extra = jnp.tile(pieces, (devices, 1))

    own_channels = lax.dynamic_slice_in_dim(channel_list, own_rank * share, share)
    omega = own_channels.astype(jnp.float32) * (TWO_PI / channels)
    theta = station_beam_lag.T[:, None, :] * omega[None, :, None]
    cosine = jnp.cos(theta)
    sine = jnp.sin(theta)
    onehot = (
        tied_beam_pointing[None, :] == jnp.arange(pointings, dtype=jnp.int32)[:, None]
    ).astype(jnp.float32)

    spectra = channel_spectra(samples, filter_taps, channel_list, extra)
    spectra = lax.all_to_all(spectra, GROUP_AXES, split_axis=0, concat_axis=0, tiled=True)
    width = 2 * frames * antennas
    total = devices * antennas

    pieces = spectra[:, width : width + groups * 3 * antennas].astype(jnp.float32)
    pieces = pieces.reshape(devices, share, groups, 3, antennas)
    info = (pieces[:, :, :, 0] + pieces[:, :, :, 1]) + pieces[:, :, :, 2]
    info = info.transpose(2, 1, 0, 3).reshape(groups * share, total)
    lag = info[:pointings]
    mask = (
        info[pointings][None, :] == jnp.arange(stations, dtype=jnp.float32)[:, None]
    ).astype(jnp.float32)
    angles = lag[None] * omega[:, None, None]
    weights = jnp.concatenate([jnp.cos(angles), jnp.sin(angles)], axis=1).astype(jnp.bfloat16)

    spectra = spectra[:, :width].reshape(devices, share, 2 * frames, antennas)
    spectra = spectra.transpose(1, 2, 0, 3).reshape(share, 2 * frames, total)
    moment_count = stations * stations - stations + 1
    power = pl.pallas_call(
        functools.partial(beam_power_kernel, frames, 1.0 / (frames * total)),
        out_shape=jax.ShapeDtypeStruct((devices, share, beams // devices), jnp.float32),
        scratch_shapes=[pltpu.VMEM((moment_count, share, pointings), jnp.float32)],
        compiler_params=pltpu.CompilerParams(vmem_limit_bytes=32 * 1024 * 1024),
    )(spectra, weights, mask, cosine, sine, onehot)
    power = lax.all_to_all(power, GROUP_AXES, split_axis=0, concat_axis=0, tiled=True)
    return power.reshape(selected, beams // devices).T


def solution(mesh):
    in_specs = (
        P(("grp", "tile", "stn"), None, None),
        P(),
        P("grp"),
        P(None, ("grp", "tile", "stn")),
        P(None, "grp"),
        P(("grp", "tile", "stn")),
        P("grp"),
        P("grp"),
        P("grp", None),
    )
    out_specs = P(("grp", "tile", "stn"), None)
    return jax.shard_map(body, mesh=mesh, in_specs=in_specs, out_specs=out_specs, check_vma=False)
```

```python
import functools
import itertools
import math

import jax
import jax.numpy as jnp
from jax import lax
from jax.experimental import pallas as pl
from jax.experimental.pallas import tpu as pltpu
from jax.sharding import PartitionSpec as P

TWO_PI = 6.283185307179586
LANES = 128
CHUNK = 512
GROUP_AXES = ("tile", "stn")


def filter_dft_kernel(frames, taps, x_ref, taps_ref, ca_ref, sa_ref, cb_ref, sb_ref, extra_ref, out_ref, filt, table, acc):
    step = pl.program_id(0)
    antennas = x_ref.shape[0]
    selected = cb_ref.shape[0]
    rows = frames * antennas

    for piece in range(CHUNK // LANES):
        lanes = slice(piece * LANES, (piece + 1) * LANES)
        ca = ca_ref[0, :, piece : piece + 1]
        sa = sa_ref[0, :, piece : piece + 1]
        cb = cb_ref[...]
        sb = sb_ref[...]
        table[0:selected, lanes] = (ca * cb - sa * sb).astype(jnp.bfloat16)
        table[selected : 2 * selected, lanes] = (sa * cb + ca * sb).astype(jnp.bfloat16)
        weights = [
            jnp.broadcast_to(taps_ref[j : j + 1, lanes], (antennas, LANES)) for j in range(taps)
        ]
        for r in range(2):
            blocks = [
                x_ref[:, k, r, lanes].astype(jnp.float32) for k in range(frames + taps - 1)
            ]
            for f in range(frames):
                total = blocks[f] * weights[0]
                for j in range(1, taps):
                    total = total + blocks[f + j] * weights[j]
                start = r * rows + f * antennas
                filt[start : start + antennas, lanes] = total.astype(jnp.bfloat16)

    product = lax.dot_general(
        table[...], filt[...], (((1,), (1,)), ((), ())), preferred_element_type=jnp.float32
    )

    @pl.when(step == 0)
    def _():
        acc[...] = product

    @pl.when(step > 0)
    def _():
        acc[...] += product

    @pl.when(step == pl.num_programs(0) - 1)
    def _():
        out_ref[:, 2 * rows :] = extra_ref[...]
        out_ref[:, 0:rows] = (
            acc[0:selected, 0:rows] + acc[selected : 2 * selected, rows : 2 * rows]
        ).astype(jnp.bfloat16)
        out_ref[:, rows : 2 * rows] = (
            acc[0:selected, rows : 2 * rows] - acc[selected : 2 * selected, 0:rows]
        ).astype(jnp.bfloat16)


def unit_tables(sample_idx, channel_list, channels, factor):
    turn_count = sample_idx * channel_list[:, None] % channels
    angles = turn_count.astype(jnp.float32) * (TWO_PI / channels)
    return jnp.cos(angles) * factor, jnp.sin(angles) * factor


def channel_spectra(samples, filter_taps, channel_list, extra):
    taps, channels = filter_taps.shape
    antennas = samples.shape[0]
    selected = channel_list.shape[0]
    blocks = samples.shape[2] // channels
    frames = blocks - taps + 1
    steps = channels // CHUNK
    pieces = CHUNK // LANES
    x = samples.reshape(antennas, 2, blocks, channels).transpose(0, 2, 1, 3)
    coarse = lax.broadcasted_iota(jnp.int32, (selected, channels // LANES), 1) * LANES
    fine = lax.broadcasted_iota(jnp.int32, (selected, LANES), 1)
    ca, sa = unit_tables(coarse, channel_list, channels, 1.0 / math.sqrt(channels))
    cb, sb = unit_tables(fine, channel_list, channels, 1.0)
    ca, sa, cb, sb = lax.optimization_barrier((ca, sa, cb, sb))
    ca = ca.reshape(selected, steps, pieces).transpose(1, 0, 2)
    sa = sa.reshape(selected, steps, pieces).transpose(1, 0, 2)
    width = 2 * frames * antennas
    return pl.pallas_call(
        functools.partial(filter_dft_kernel, frames, taps),
        grid=(steps,),
        in_specs=[
            pl.BlockSpec((antennas, blocks, 2, CHUNK), lambda i: (0, 0, 0, i)),
            pl.BlockSpec((taps, CHUNK), lambda i: (0, i)),
            pl.BlockSpec((1, selected, pieces), lambda i: (i, 0, 0)),
            pl.BlockSpec((1, selected, pieces), lambda i: (i, 0, 0)),
            pl.BlockSpec((selected, LANES), lambda i: (0, 0)),
            pl.BlockSpec((selected, LANES), lambda i: (0, 0)),
            pl.BlockSpec(extra.shape, lambda i: (0, 0)),
        ],
        out_specs=pl.BlockSpec((selected, width + extra.shape[1]), lambda i: (0, 0)),
        out_shape=jax.ShapeDtypeStruct((selected, width + extra.shape[1]), jnp.bfloat16),
        scratch_shapes=[
            pltpu.VMEM((width, CHUNK), jnp.bfloat16),
            pltpu.VMEM((2 * selected, CHUNK), jnp.bfloat16),
            pltpu.VMEM((2 * selected, width), jnp.float32),
        ],
        compiler_params=pltpu.CompilerParams(vmem_limit_bytes=32 * 1024 * 1024),
    )(x, filter_taps, ca, sa, cb, sb, extra)


def beam_power_kernel(frames, factor, x_ref, w_ref, mask_ref, cos_ref, sin_ref, onehot_ref, out_ref, moments):
    share = x_ref.shape[0]
    stations = mask_ref.shape[0]
    pointings = onehot_ref.shape[0]
    pairs = list(itertools.combinations(range(stations), 2))
    for c in range(share):
        x = x_ref[c].astype(jnp.float32)
        real, imag = [], []
        for s in range(stations):
            masked = (x * mask_ref[s : s + 1, :]).astype(jnp.bfloat16)
            terms = lax.dot_general(
                masked, w_ref[c], (((1,), (1,)), ((), ())), preferred_element_type=jnp.float32
            )
            cos_part = terms[:, 0:pointings]
            sin_part = terms[:, pointings : 2 * pointings]
            real.append(cos_part[0:frames] + sin_part[frames : 2 * frames])
            imag.append(cos_part[frames : 2 * frames] - sin_part[0:frames])
        total = real[0] * real[0] + imag[0] * imag[0]
        for s in range(1, stations):
            total = total + (real[s] * real[s] + imag[s] * imag[s])
        moments[0, c : c + 1, :] = jnp.sum(total, axis=0, keepdims=True) * factor
        for i, (s, t) in enumerate(pairs):
            even = real[s] * real[t] + imag[s] * imag[t]
            odd = imag[s] * real[t] - real[s] * imag[t]
            moments[1 + i, c : c + 1, :] = jnp.sum(even, axis=0, keepdims=True) * (2.0 * factor)
            moments[1 + len(pairs) + i, c : c + 1, :] = jnp.sum(odd, axis=0, keepdims=True) * (
                2.0 * factor
            )

    def chosen(m):
        return jnp.dot(
            moments[m],
            onehot_ref[...],
            precision=lax.Precision.HIGHEST,
            preferred_element_type=jnp.float32,
        )

    power = chosen(0)
    for i, (s, t) in enumerate(pairs):
        power = power + chosen(1 + i) * (cos_ref[s] * cos_ref[t] + sin_ref[s] * sin_ref[t])
        power = power + chosen(1 + len(pairs) + i) * (
            sin_ref[s] * cos_ref[t] - cos_ref[s] * sin_ref[t]
        )
    beams = out_ref.shape[2]
    for d in range(out_ref.shape[0]):
        out_ref[d] = power[:, d * beams : (d + 1) * beams]


def split_rows(values):
    first = lax.reduce_precision(values, 8, 7)
    second = lax.reduce_precision(values - first, 8, 7)
    third = values - first - second
    return jnp.stack([first, second, third], axis=1).astype(jnp.bfloat16)


def antenna_info(antenna_tile_lag, tile_station_lag, tile_of_antenna, tile_station):
    tile_ids = jnp.arange(tile_station_lag.shape[1], dtype=jnp.int32)
    matches = tile_of_antenna[:, None] == tile_ids[None, :]
    extra = jnp.sum(jnp.where(matches[None, :, :], tile_station_lag[:, None, :], 0.0), axis=2)
    station = jnp.sum(jnp.where(matches, tile_station[None, :], 0), axis=1)
    return jnp.concatenate([antenna_tile_lag + extra, station.astype(jnp.float32)[None]], axis=0)


def body(
    samples,
    filter_taps,
    channel_list,
    antenna_tile_lag,
    tile_station_lag,
    tile_of_antenna,
    tile_station,
    tied_beam_pointing,
    station_beam_lag,
):
    devices = lax.axis_size(GROUP_AXES)
    own_rank = lax.axis_index(GROUP_AXES)
    taps, channels = filter_taps.shape
    frames = samples.shape[2] // channels - taps + 1
    stations = station_beam_lag.shape[1]
    pointings = tile_station_lag.shape[0]
    selected = channel_list.shape[0]
    antennas = samples.shape[0]
    share = selected // devices
    beams = tied_beam_pointing.shape[0]

    info = antenna_info(antenna_tile_lag, tile_station_lag, tile_of_antenna, tile_station)
    info_rows = info.shape[0]
    groups = -(-info_rows // share)
    pieces = split_rows(info)
    pieces = jnp.pad(pieces, ((0, groups * share - info_rows), (0, 0), (0, 0)))
    pieces = pieces.reshape(groups, share, 3 * antennas).transpose(1, 0, 2)
    pieces = pieces.reshape(share, groups * 3 * antennas)
    extra_width = -(-pieces.shape[1] // LANES) * LANES
    pieces = jnp.pad(pieces, ((0, 0), (0, extra_width - pieces.shape[1])))
    extra = jnp.tile(pieces, (devices, 1))

    own_channels = lax.dynamic_slice_in_dim(channel_list, own_rank * share, share)
    omega = own_channels.astype(jnp.float32) * (TWO_PI / channels)
    theta = station_beam_lag.T[:, None, :] * omega[None, :, None]
    cosine = jnp.cos(theta)
    sine = jnp.sin(theta)
    onehot = (
        tied_beam_pointing[None, :] == jnp.arange(pointings, dtype=jnp.int32)[:, None]
    ).astype(jnp.float32)

    spectra = channel_spectra(samples, filter_taps, channel_list, extra)
    spectra = lax.all_to_all(spectra, GROUP_AXES, split_axis=0, concat_axis=0, tiled=True)
    width = 2 * frames * antennas
    total = devices * antennas

    pieces = spectra[:, width : width + groups * 3 * antennas].astype(jnp.float32)
    pieces = pieces.reshape(devices, share, groups, 3, antennas)
    info = (pieces[:, :, :, 0] + pieces[:, :, :, 1]) + pieces[:, :, :, 2]
    info = info.transpose(2, 1, 0, 3).reshape(groups * share, total)
    lag = info[:pointings]
    mask = (
        info[pointings][None, :] == jnp.arange(stations, dtype=jnp.float32)[:, None]
    ).astype(jnp.float32)
    angles = lag[None] * omega[:, None, None]
    weights = jnp.concatenate([jnp.cos(angles), jnp.sin(angles)], axis=1).astype(jnp.bfloat16)

    spectra = spectra[:, :width].reshape(devices, share, 2 * frames, antennas)
    spectra = spectra.transpose(1, 2, 0, 3).reshape(share, 2 * frames, total)
    moment_count = stations * stations - stations + 1
    power = pl.pallas_call(
        functools.partial(beam_power_kernel, frames, 1.0 / (frames * total)),
        out_shape=jax.ShapeDtypeStruct((devices, share, beams // devices), jnp.float32),
        scratch_shapes=[pltpu.VMEM((moment_count, share, pointings), jnp.float32)],
        compiler_params=pltpu.CompilerParams(vmem_limit_bytes=32 * 1024 * 1024),
    )(spectra, weights, mask, cosine, sine, onehot)
    power = lax.all_to_all(power, GROUP_AXES, split_axis=0, concat_axis=0, tiled=True)
    return power.reshape(selected, beams // devices).T


def solution(mesh):
    in_specs = (
        P(("grp", "tile", "stn"), None, None),
        P(),
        P("grp"),
        P(None, ("grp", "tile", "stn")),
        P(None, "grp"),
        P(("grp", "tile", "stn")),
        P("grp"),
        P("grp"),
        P("grp", None),
    )
    out_specs = P(("grp", "tile", "stn"), None)
    return jax.shard_map(body, mesh=mesh, in_specs=in_specs, out_specs=out_specs, check_vma=False)
```

```python
import functools
import itertools
import math

import jax
import jax.numpy as jnp
from jax import lax
from jax.experimental import pallas as pl
from jax.experimental.pallas import tpu as pltpu
from jax.sharding import PartitionSpec as P

TWO_PI = 6.283185307179586
LANES = 128
CHUNK = 512
GROUP_AXES = ("tile", "stn")


def filter_dft_kernel(frames, taps, x_ref, taps_ref, ca_ref, sa_ref, cb_ref, sb_ref, extra_ref, out_ref, filt, mixed, table, acc):
    step = pl.program_id(0)
    antennas = x_ref.shape[0]
    selected = cb_ref.shape[0]
    rows = frames * antennas

    for piece in range(CHUNK // LANES):
        lanes = slice(piece * LANES, (piece + 1) * LANES)
        ca = ca_ref[0, :, piece : piece + 1]
        sa = sa_ref[0, :, piece : piece + 1]
        cb = cb_ref[...]
        sb = sb_ref[...]
        table[0:selected, lanes] = (ca * cb - sa * sb).astype(jnp.bfloat16)
        table[selected : 2 * selected, lanes] = (sa * cb + ca * sb).astype(jnp.bfloat16)
        weights = [
            jnp.broadcast_to(taps_ref[j : j + 1, lanes], (2 * antennas, LANES))
            for j in range(taps)
        ]
        blocks = [
            x_ref[:, k, :, lanes].reshape(2 * antennas, LANES).astype(jnp.float32)
            for k in range(frames + taps - 1)
        ]
        for f in range(frames):
            total = blocks[f] * weights[0]
            for j in range(1, taps):
                total = total + blocks[f + j] * weights[j]
            mixed[f] = total
            for r in range(2):
                start = r * rows + f * antennas
                filt[start : start + antennas, lanes] = mixed[
                    f, pl.ds(r, antennas, stride=2), :
                ].astype(jnp.bfloat16)

    product = lax.dot_general(
        table[...], filt[...], (((1,), (1,)), ((), ())), preferred_element_type=jnp.float32
    )

    @pl.when(step == 0)
    def _():
        acc[...] = product

    @pl.when(step > 0)
    def _():
        acc[...] += product

    @pl.when(step == pl.num_programs(0) - 1)
    def _():
        out_ref[:, 2 * rows :] = extra_ref[...]
        out_ref[:, 0:rows] = (
            acc[0:selected, 0:rows] + acc[selected : 2 * selected, rows : 2 * rows]
        ).astype(jnp.bfloat16)
        out_ref[:, rows : 2 * rows] = (
            acc[0:selected, rows : 2 * rows] - acc[selected : 2 * selected, 0:rows]
        ).astype(jnp.bfloat16)


def unit_tables(sample_idx, channel_list, channels, factor):
    turn_count = sample_idx * channel_list[:, None] % channels
    angles = turn_count.astype(jnp.float32) * (TWO_PI / channels)
    return jnp.cos(angles) * factor, jnp.sin(angles) * factor


def channel_spectra(samples, filter_taps, channel_list, extra):
    taps, channels = filter_taps.shape
    antennas = samples.shape[0]
    selected = channel_list.shape[0]
    blocks = samples.shape[2] // channels
    frames = blocks - taps + 1
    steps = channels // CHUNK
    pieces = CHUNK // LANES
    x = samples.reshape(antennas, 2, blocks, channels).transpose(0, 2, 1, 3)
    coarse = lax.broadcasted_iota(jnp.int32, (selected, channels // LANES), 1) * LANES
    fine = lax.broadcasted_iota(jnp.int32, (selected, LANES), 1)
    ca, sa = unit_tables(coarse, channel_list, channels, 1.0 / math.sqrt(channels))
    cb, sb = unit_tables(fine, channel_list, channels, 1.0)
    ca, sa, cb, sb = lax.optimization_barrier((ca, sa, cb, sb))
    ca = ca.reshape(selected, steps, pieces).transpose(1, 0, 2)
    sa = sa.reshape(selected, steps, pieces).transpose(1, 0, 2)
    width = 2 * frames * antennas
    return pl.pallas_call(
        functools.partial(filter_dft_kernel, frames, taps),
        grid=(steps,),
        in_specs=[
            pl.BlockSpec((antennas, blocks, 2, CHUNK), lambda i: (0, 0, 0, i)),
            pl.BlockSpec((taps, CHUNK), lambda i: (0, i)),
            pl.BlockSpec((1, selected, pieces), lambda i: (i, 0, 0)),
            pl.BlockSpec((1, selected, pieces), lambda i: (i, 0, 0)),
            pl.BlockSpec((selected, LANES), lambda i: (0, 0)),
            pl.BlockSpec((selected, LANES), lambda i: (0, 0)),
            pl.BlockSpec(extra.shape, lambda i: (0, 0)),
        ],
        out_specs=pl.BlockSpec((selected, width + extra.shape[1]), lambda i: (0, 0)),
        out_shape=jax.ShapeDtypeStruct((selected, width + extra.shape[1]), jnp.bfloat16),
        scratch_shapes=[
            pltpu.VMEM((width, CHUNK), jnp.bfloat16),
            pltpu.VMEM((frames, 2 * antennas, LANES), jnp.float32),
            pltpu.VMEM((2 * selected, CHUNK), jnp.bfloat16),
            pltpu.VMEM((2 * selected, width), jnp.float32),
        ],
        compiler_params=pltpu.CompilerParams(vmem_limit_bytes=32 * 1024 * 1024),
    )(x, filter_taps, ca, sa, cb, sb, extra)


def beam_power_kernel(frames, factor, x_ref, w_ref, mask_ref, cos_ref, sin_ref, onehot_ref, out_ref, moments):
    share = x_ref.shape[0]
    stations = mask_ref.shape[0]
    pointings = onehot_ref.shape[0]
    pairs = list(itertools.combinations(range(stations), 2))
    for c in range(share):
        x = x_ref[c].astype(jnp.float32)
        real, imag = [], []
        for s in range(stations):
            masked = (x * mask_ref[s : s + 1, :]).astype(jnp.bfloat16)
            terms = lax.dot_general(
                masked, w_ref[c], (((1,), (1,)), ((), ())), preferred_element_type=jnp.float32
            )
            cos_part = terms[:, 0:pointings]
            sin_part = terms[:, pointings : 2 * pointings]
            real.append(cos_part[0:frames] + sin_part[frames : 2 * frames])
            imag.append(cos_part[frames : 2 * frames] - sin_part[0:frames])
        total = real[0] * real[0] + imag[0] * imag[0]
        for s in range(1, stations):
            total = total + (real[s] * real[s] + imag[s] * imag[s])
        moments[0, c : c + 1, :] = jnp.sum(total, axis=0, keepdims=True) * factor
        for i, (s, t) in enumerate(pairs):
            even = real[s] * real[t] + imag[s] * imag[t]
            odd = imag[s] * real[t] - real[s] * imag[t]
            moments[1 + i, c : c + 1, :] = jnp.sum(even, axis=0, keepdims=True) * (2.0 * factor)
            moments[1 + len(pairs) + i, c : c + 1, :] = jnp.sum(odd, axis=0, keepdims=True) * (
                2.0 * factor
            )

    def chosen(m):
        return jnp.dot(
            moments[m],
            onehot_ref[...],
            precision=lax.Precision.HIGHEST,
            preferred_element_type=jnp.float32,
        )

    power = chosen(0)
    for i, (s, t) in enumerate(pairs):
        power = power + chosen(1 + i) * (cos_ref[s] * cos_ref[t] + sin_ref[s] * sin_ref[t])
        power = power + chosen(1 + len(pairs) + i) * (
            sin_ref[s] * cos_ref[t] - cos_ref[s] * sin_ref[t]
        )
    beams = out_ref.shape[2]
    for d in range(out_ref.shape[0]):
        out_ref[d] = power[:, d * beams : (d + 1) * beams]


def split_rows(values):
    first = lax.reduce_precision(values, 8, 7)
    second = lax.reduce_precision(values - first, 8, 7)
    third = values - first - second
    return jnp.stack([first, second, third], axis=1).astype(jnp.bfloat16)


def antenna_info(antenna_tile_lag, tile_station_lag, tile_of_antenna, tile_station):
    tile_ids = jnp.arange(tile_station_lag.shape[1], dtype=jnp.int32)
    matches = tile_of_antenna[:, None] == tile_ids[None, :]
    extra = jnp.sum(jnp.where(matches[None, :, :], tile_station_lag[:, None, :], 0.0), axis=2)
    station = jnp.sum(jnp.where(matches, tile_station[None, :], 0), axis=1)
    return jnp.concatenate([antenna_tile_lag + extra, station.astype(jnp.float32)[None]], axis=0)


def body(
    samples,
    filter_taps,
    channel_list,
    antenna_tile_lag,
    tile_station_lag,
    tile_of_antenna,
    tile_station,
    tied_beam_pointing,
    station_beam_lag,
):
    devices = lax.axis_size(GROUP_AXES)
    own_rank = lax.axis_index(GROUP_AXES)
    taps, channels = filter_taps.shape
    frames = samples.shape[2] // channels - taps + 1
    stations = station_beam_lag.shape[1]
    pointings = tile_station_lag.shape[0]
    selected = channel_list.shape[0]
    antennas = samples.shape[0]
    share = selected // devices
    beams = tied_beam_pointing.shape[0]

    info = antenna_info(antenna_tile_lag, tile_station_lag, tile_of_antenna, tile_station)
    info_rows = info.shape[0]
    groups = -(-info_rows // share)
    pieces = split_rows(info)
    pieces = jnp.pad(pieces, ((0, groups * share - info_rows), (0, 0), (0, 0)))
    pieces = pieces.reshape(groups, share, 3 * antennas).transpose(1, 0, 2)
    pieces = pieces.reshape(share, groups * 3 * antennas)
    extra_width = -(-pieces.shape[1] // LANES) * LANES
    pieces = jnp.pad(pieces, ((0, 0), (0, extra_width - pieces.shape[1])))
    extra = jnp.tile(pieces, (devices, 1))

    own_channels = lax.dynamic_slice_in_dim(channel_list, own_rank * share, share)
    omega = own_channels.astype(jnp.float32) * (TWO_PI / channels)
    theta = station_beam_lag.T[:, None, :] * omega[None, :, None]
    cosine = jnp.cos(theta)
    sine = jnp.sin(theta)
    onehot = (
        tied_beam_pointing[None, :] == jnp.arange(pointings, dtype=jnp.int32)[:, None]
    ).astype(jnp.float32)

    spectra = channel_spectra(samples, filter_taps, channel_list, extra)
    spectra = lax.all_to_all(spectra, GROUP_AXES, split_axis=0, concat_axis=0, tiled=True)
    width = 2 * frames * antennas
    total = devices * antennas

    pieces = spectra[:, width : width + groups * 3 * antennas].astype(jnp.float32)
    pieces = pieces.reshape(devices, share, groups, 3, antennas)
    info = (pieces[:, :, :, 0] + pieces[:, :, :, 1]) + pieces[:, :, :, 2]
    info = info.transpose(2, 1, 0, 3).reshape(groups * share, total)
    lag = info[:pointings]
    mask = (
        info[pointings][None, :] == jnp.arange(stations, dtype=jnp.float32)[:, None]
    ).astype(jnp.float32)
    angles = lag[None] * omega[:, None, None]
    weights = jnp.concatenate([jnp.cos(angles), jnp.sin(angles)], axis=1).astype(jnp.bfloat16)

    spectra = spectra[:, :width].reshape(devices, share, 2 * frames, antennas)
    spectra = spectra.transpose(1, 2, 0, 3).reshape(share, 2 * frames, total)
    moment_count = stations * stations - stations + 1
    power = pl.pallas_call(
        functools.partial(beam_power_kernel, frames, 1.0 / (frames * total)),
        out_shape=jax.ShapeDtypeStruct((devices, share, beams // devices), jnp.float32),
        scratch_shapes=[pltpu.VMEM((moment_count, share, pointings), jnp.float32)],
        compiler_params=pltpu.CompilerParams(vmem_limit_bytes=32 * 1024 * 1024),
    )(spectra, weights, mask, cosine, sine, onehot)
    power = lax.all_to_all(power, GROUP_AXES, split_axis=0, concat_axis=0, tiled=True)
    return power.reshape(selected, beams // devices).T


def solution(mesh):
    in_specs = (
        P(("grp", "tile", "stn"), None, None),
        P(),
        P("grp"),
        P(None, ("grp", "tile", "stn")),
        P(None, "grp"),
        P(("grp", "tile", "stn")),
        P("grp"),
        P("grp"),
        P("grp", None),
    )
    out_specs = P(("grp", "tile", "stn"), None)
    return jax.shard_map(body, mesh=mesh, in_specs=in_specs, out_specs=out_specs, check_vma=False)
```

```python
import functools
import itertools
import math

import jax
import jax.numpy as jnp
from jax import lax
from jax.experimental import pallas as pl
from jax.experimental.pallas import tpu as pltpu
from jax.sharding import PartitionSpec as P

TWO_PI = 6.283185307179586
LANES = 128
CHUNK = 512
GROUP_AXES = ("tile", "stn")


def filter_dft_kernel(frames, taps, x_ref, taps_ref, ca_ref, sa_ref, cb_ref, sb_ref, extra_ref, out_ref, filt, table, acc):
    step = pl.program_id(0)
    antennas = x_ref.shape[0]
    selected = cb_ref.shape[0]
    rows = frames * antennas

    for piece in range(CHUNK // LANES):
        lanes = slice(piece * LANES, (piece + 1) * LANES)
        ca = ca_ref[0, :, piece : piece + 1]
        sa = sa_ref[0, :, piece : piece + 1]
        cb = cb_ref[...]
        sb = sb_ref[...]
        table[0:selected, lanes] = (ca * cb - sa * sb).astype(jnp.bfloat16)
        table[selected : 2 * selected, lanes] = (sa * cb + ca * sb).astype(jnp.bfloat16)
        weights = [
            jnp.broadcast_to(taps_ref[j : j + 1, lanes], (antennas, LANES)) for j in range(taps)
        ]
        for r in range(2):
            blocks = [
                x_ref[:, k, r, lanes].astype(jnp.float32) for k in range(frames + taps - 1)
            ]
            for f in range(frames):
                total = blocks[f] * weights[0]
                for j in range(1, taps):
                    total = total + blocks[f + j] * weights[j]
                start = r * rows + f * antennas
                filt[start : start + antennas, lanes] = total.astype(jnp.bfloat16)

    product = lax.dot_general(
        table[...], filt[...], (((1,), (1,)), ((), ())), preferred_element_type=jnp.float32
    )

    @pl.when(step == 0)
    def _():
        acc[...] = product

    @pl.when(step > 0)
    def _():
        acc[...] += product

    @pl.when(step == pl.num_programs(0) - 1)
    def _():
        out_ref[:, 2 * rows :] = extra_ref[...]
        out_ref[:, 0:rows] = (
            acc[0:selected, 0:rows] + acc[selected : 2 * selected, rows : 2 * rows]
        ).astype(jnp.bfloat16)
        out_ref[:, rows : 2 * rows] = (
            acc[0:selected, rows : 2 * rows] - acc[selected : 2 * selected, 0:rows]
        ).astype(jnp.bfloat16)


def unit_tables(sample_idx, channel_list, channels, factor):
    turn_count = sample_idx * channel_list[:, None] % channels
    angles = turn_count.astype(jnp.float32) * (TWO_PI / channels)
    return jnp.cos(angles) * factor, jnp.sin(angles) * factor


def channel_spectra(samples, filter_taps, channel_list, extra):
    taps, channels = filter_taps.shape
    antennas = samples.shape[0]
    selected = channel_list.shape[0]
    blocks = samples.shape[2] // channels
    frames = blocks - taps + 1
    steps = channels // CHUNK
    pieces = CHUNK // LANES
    x = samples.reshape(antennas, 2, blocks, channels).transpose(0, 2, 1, 3)
    coarse = lax.broadcasted_iota(jnp.int32, (selected, channels // LANES), 1) * LANES
    fine = lax.broadcasted_iota(jnp.int32, (selected, LANES), 1)
    ca, sa = unit_tables(coarse, channel_list, channels, 1.0 / math.sqrt(channels))
    cb, sb = unit_tables(fine, channel_list, channels, 1.0)
    ca, sa, cb, sb = lax.optimization_barrier((ca, sa, cb, sb))
    ca = ca.reshape(selected, steps, pieces).transpose(1, 0, 2)
    sa = sa.reshape(selected, steps, pieces).transpose(1, 0, 2)
    width = 2 * frames * antennas
    return pl.pallas_call(
        functools.partial(filter_dft_kernel, frames, taps),
        grid=(steps,),
        in_specs=[
            pl.BlockSpec((antennas, blocks, 2, CHUNK), lambda i: (0, 0, 0, i)),
            pl.BlockSpec((taps, CHUNK), lambda i: (0, i)),
            pl.BlockSpec((1, selected, pieces), lambda i: (i, 0, 0)),
            pl.BlockSpec((1, selected, pieces), lambda i: (i, 0, 0)),
            pl.BlockSpec((selected, LANES), lambda i: (0, 0)),
            pl.BlockSpec((selected, LANES), lambda i: (0, 0)),
            pl.BlockSpec(extra.shape, lambda i: (0, 0)),
        ],
        out_specs=pl.BlockSpec((selected, width + extra.shape[1]), lambda i: (0, 0)),
        out_shape=jax.ShapeDtypeStruct((selected, width + extra.shape[1]), jnp.bfloat16),
        scratch_shapes=[
            pltpu.VMEM((width, CHUNK), jnp.bfloat16),
            pltpu.VMEM((2 * selected, CHUNK), jnp.bfloat16),
            pltpu.VMEM((2 * selected, width), jnp.float32),
        ],
        compiler_params=pltpu.CompilerParams(vmem_limit_bytes=60 * 1024 * 1024),
    )(x, filter_taps, ca, sa, cb, sb, extra)


def beam_power_kernel(frames, factor, x_ref, w_ref, mask_ref, cos_ref, sin_ref, onehot_ref, out_ref, moments):
    share = x_ref.shape[0]
    stations = mask_ref.shape[0]
    pointings = onehot_ref.shape[0]
    pairs = list(itertools.combinations(range(stations), 2))
    for c in range(share):
        x = x_ref[c].astype(jnp.float32)
        real, imag = [], []
        for s in range(stations):
            masked = (x * mask_ref[s : s + 1, :]).astype(jnp.bfloat16)
            terms = lax.dot_general(
                masked, w_ref[c], (((1,), (1,)), ((), ())), preferred_element_type=jnp.float32
            )
            cos_part = terms[:, 0:pointings]
            sin_part = terms[:, pointings : 2 * pointings]
            real.append(cos_part[0:frames] + sin_part[frames : 2 * frames])
            imag.append(cos_part[frames : 2 * frames] - sin_part[0:frames])
        total = real[0] * real[0] + imag[0] * imag[0]
        for s in range(1, stations):
            total = total + (real[s] * real[s] + imag[s] * imag[s])
        moments[0, c : c + 1, :] = jnp.sum(total, axis=0, keepdims=True) * factor
        for i, (s, t) in enumerate(pairs):
            even = real[s] * real[t] + imag[s] * imag[t]
            odd = imag[s] * real[t] - real[s] * imag[t]
            moments[1 + i, c : c + 1, :] = jnp.sum(even, axis=0, keepdims=True) * (2.0 * factor)
            moments[1 + len(pairs) + i, c : c + 1, :] = jnp.sum(odd, axis=0, keepdims=True) * (
                2.0 * factor
            )

    def chosen(m):
        return jnp.dot(
            moments[m],
            onehot_ref[...],
            precision=lax.Precision.HIGHEST,
            preferred_element_type=jnp.float32,
        )

    power = chosen(0)
    for i, (s, t) in enumerate(pairs):
        power = power + chosen(1 + i) * (cos_ref[s] * cos_ref[t] + sin_ref[s] * sin_ref[t])
        power = power + chosen(1 + len(pairs) + i) * (
            sin_ref[s] * cos_ref[t] - cos_ref[s] * sin_ref[t]
        )
    beams = out_ref.shape[2]
    for d in range(out_ref.shape[0]):
        out_ref[d] = power[:, d * beams : (d + 1) * beams]


def split_rows(values):
    first = lax.reduce_precision(values, 8, 7)
    second = lax.reduce_precision(values - first, 8, 7)
    third = values - first - second
    return jnp.stack([first, second, third], axis=1).astype(jnp.bfloat16)


def antenna_info(antenna_tile_lag, tile_station_lag, tile_of_antenna, tile_station):
    tile_ids = jnp.arange(tile_station_lag.shape[1], dtype=jnp.int32)
    matches = tile_of_antenna[:, None] == tile_ids[None, :]
    extra = jnp.sum(jnp.where(matches[None, :, :], tile_station_lag[:, None, :], 0.0), axis=2)
    station = jnp.sum(jnp.where(matches, tile_station[None, :], 0), axis=1)
    return jnp.concatenate([antenna_tile_lag + extra, station.astype(jnp.float32)[None]], axis=0)


def body(
    samples,
    filter_taps,
    channel_list,
    antenna_tile_lag,
    tile_station_lag,
    tile_of_antenna,
    tile_station,
    tied_beam_pointing,
    station_beam_lag,
):
    devices = lax.axis_size(GROUP_AXES)
    own_rank = lax.axis_index(GROUP_AXES)
    taps, channels = filter_taps.shape
    frames = samples.shape[2] // channels - taps + 1
    stations = station_beam_lag.shape[1]
    pointings = tile_station_lag.shape[0]
    selected = channel_list.shape[0]
    antennas = samples.shape[0]
    share = selected // devices
    beams = tied_beam_pointing.shape[0]

    info = antenna_info(antenna_tile_lag, tile_station_lag, tile_of_antenna, tile_station)
    info_rows = info.shape[0]
    groups = -(-info_rows // share)
    pieces = split_rows(info)
    pieces = jnp.pad(pieces, ((0, groups * share - info_rows), (0, 0), (0, 0)))
    pieces = pieces.reshape(groups, share, 3 * antennas).transpose(1, 0, 2)
    pieces = pieces.reshape(share, groups * 3 * antennas)
    extra_width = -(-pieces.shape[1] // LANES) * LANES
    pieces = jnp.pad(pieces, ((0, 0), (0, extra_width - pieces.shape[1])))
    extra = jnp.tile(pieces, (devices, 1))

    own_channels = lax.dynamic_slice_in_dim(channel_list, own_rank * share, share)
    omega = own_channels.astype(jnp.float32) * (TWO_PI / channels)
    theta = station_beam_lag.T[:, None, :] * omega[None, :, None]
    cosine = jnp.cos(theta)
    sine = jnp.sin(theta)
    onehot = (
        tied_beam_pointing[None, :] == jnp.arange(pointings, dtype=jnp.int32)[:, None]
    ).astype(jnp.float32)

    spectra = channel_spectra(samples, filter_taps, channel_list, extra)
    spectra = lax.all_to_all(spectra, GROUP_AXES, split_axis=0, concat_axis=0, tiled=True)
    width = 2 * frames * antennas
    total = devices * antennas

    pieces = spectra[:, width : width + groups * 3 * antennas].astype(jnp.float32)
    pieces = pieces.reshape(devices, share, groups, 3, antennas)
    info = (pieces[:, :, :, 0] + pieces[:, :, :, 1]) + pieces[:, :, :, 2]
    info = info.transpose(2, 1, 0, 3).reshape(groups * share, total)
    lag = info[:pointings]
    mask = (
        info[pointings][None, :] == jnp.arange(stations, dtype=jnp.float32)[:, None]
    ).astype(jnp.float32)
    angles = lag[None] * omega[:, None, None]
    weights = jnp.concatenate([jnp.cos(angles), jnp.sin(angles)], axis=1).astype(jnp.bfloat16)

    spectra = spectra[:, :width].reshape(devices, share, 2 * frames, antennas)
    spectra = spectra.transpose(1, 2, 0, 3).reshape(share, 2 * frames, total)
    moment_count = stations * stations - stations + 1
    power = pl.pallas_call(
        functools.partial(beam_power_kernel, frames, 1.0 / (frames * total)),
        out_shape=jax.ShapeDtypeStruct((devices, share, beams // devices), jnp.float32),
        scratch_shapes=[pltpu.VMEM((moment_count, share, pointings), jnp.float32)],
        compiler_params=pltpu.CompilerParams(vmem_limit_bytes=32 * 1024 * 1024),
    )(spectra, weights, mask, cosine, sine, onehot)
    power = lax.all_to_all(power, GROUP_AXES, split_axis=0, concat_axis=0, tiled=True)
    return power.reshape(selected, beams // devices).T


def solution(mesh):
    in_specs = (
        P(("grp", "tile", "stn"), None, None),
        P(),
        P("grp"),
        P(None, ("grp", "tile", "stn")),
        P(None, "grp"),
        P(("grp", "tile", "stn")),
        P("grp"),
        P("grp"),
        P("grp", None),
    )
    out_specs = P(("grp", "tile", "stn"), None)
    return jax.shard_map(body, mesh=mesh, in_specs=in_specs, out_specs=out_specs, check_vma=False)
```
